32 devices in a mesh: ctx: 16 (over z, y, core), ch: 2 (over x).
Axes of the slice: x: 2, y: 2, z: 4, core: 2. Of those that a mesh axis runs over, the one named last changes fastest.
Arguments:
- inputs: bfloat16 [2048, 4096], P('ctx', 'ch'), may hold values from -0.125 to 0.125
- out_grad: bfloat16 [2048, 4096], P('ctx', 'ch'), may hold values from -6 to 6
- filter_taps: bfloat16 [512, 4096], P('ctx', 'ch'), may hold values from -0.25 to 0.25
- skip_gain: float32 [4096], P('ch'), may hold values from 0.3 to 3
Outputs:
- input_grad: float32 [2048, 4096], P('ctx', 'ch')
- filter_grad: float32 [512, 4096], P('ctx', 'ch')
The draws below stay inside these ranges and needn't reach their ends.
All inputs are finite; a program needn't handle non-finite values.
Results may differ from the reference program's by a relative error of at most 0.0003.
Values may be sent and summed in bfloat16 or wider, within the bound.
A program may use at most 128 MiB of HBM per device.

```python
import math
import jax
import jax.numpy as jnp
from jax import lax

WIDTH = 4096
TOKENS = 2048
TAPS = 512


def block_levels(own_key, dims, pieces, least, high):
    gain = 1.0
    for position, blocks in pieces:
        steps = jax.random.uniform(jax.random.fold_in(jax.random.fold_in(own_key, 6), position), (blocks,), jnp.float32, least / len(pieces), high / len(pieces))
        gain = gain * jnp.repeat(jnp.exp(steps), dims[position] // blocks).reshape((-1,) + (1,) * (len(dims) - 1 - position))
    return gain


def normal_values(stream_key, dims, width, bound, split=(), held_as=jnp.bfloat16):
    drawn = jax.random.normal(stream_key, dims, jnp.float32) * width
    if len(split) > 0:
        drawn = block_levels(stream_key, dims, split, -0.22, 0.18) * drawn
    return jnp.clip(drawn, min=-bound, max=bound).astype(held_as)


def setup_inputs(seed: int = 0) -> dict:
    keys = jax.random.split(jax.random.key(seed), 5)
    inputs = normal_values(keys[0], (TOKENS, WIDTH), (1.0 / TOKENS ** 0.5), 0.125, ((0, 16), (1, 2)))
    out_grad = normal_values(keys[1], (TOKENS, WIDTH), 1.0, 6.0, ((0, 16), (1, 2)))
    filter_taps = normal_values(keys[2], (TAPS, WIDTH), TAPS ** -0.5, 0.25, ((0, 16), (1, 2)))
    skip_gain = jnp.clip(jnp.exp(math.log(3.0) - 2.3025851 * jax.random.uniform(keys[3], (WIDTH,), jnp.float32) ** block_levels(keys[3], (WIDTH,), ((0, 2),), -0.2, 0.2)), 0.3, 3.0)
    return dict(inputs=inputs, out_grad=out_grad, filter_taps=filter_taps, skip_gain=skip_gain)


def reference(inputs, out_grad, filter_taps, skip_gain):
    groups = WIDTH // 512 if WIDTH >= 512 else 1
    fft_size = 2 * TOKENS

    def regroup(array, rows):
        return array.astype(jnp.float32).reshape(rows, groups, WIDTH // groups).transpose(1, 0, 2)

    def one_group(operands):
        signal, gradient, kernel = operands
        grad_rev = jnp.fft.rfft(gradient[::-1], fft_size, axis=0)
        conv_rev = jnp.fft.irfft(jnp.fft.rfft(kernel, fft_size, axis=0) * grad_rev, fft_size, axis=0)[:TOKENS]
        full_corr = jnp.fft.irfft(jnp.fft.rfft(signal, fft_size, axis=0) * grad_rev, fft_size, axis=0)
        return conv_rev[::-1], full_corr[TOKENS - TAPS:TOKENS][::-1]

    conv_part, taps_grad = lax.map(one_group, (regroup(inputs, TOKENS), regroup(out_grad, TOKENS), regroup(filter_taps, TAPS)))
    conv_part = conv_part.transpose(1, 0, 2).reshape(TOKENS, WIDTH)
    taps_grad = taps_grad.transpose(1, 0, 2).reshape(TAPS, WIDTH)
    input_grad = skip_gain[None, :] * out_grad.astype(jnp.float32) + conv_part
    return input_grad.astype(jnp.float32), taps_grad.astype(jnp.float32)
```

```python
import functools

import jax
import jax.numpy as jnp
import numpy as np
from jax import lax
from jax.experimental import pallas as pl
from jax.experimental.pallas import tpu as pltpu
from jax.sharding import PartitionSpec as P

MESH = pl.DeviceIdType.MESH


def split_table(table):
    high = table.astype(jnp.bfloat16)
    low = (table - high.astype(np.float64)).astype(jnp.bfloat16)
    return np.concatenate([high, low], axis=1)


def tables(block):
    window = 2 * block
    odd = 2 * np.arange(block, dtype=np.int64)[:, None] + 1
    places = np.arange(window, dtype=np.int64)[None, :]
    angle = np.pi / window * (odd * places % (2 * window)).astype(np.float64)
    forward = np.concatenate([np.cos(angle), -np.sin(angle)], axis=0)
    inverse = forward[:, :block].T / block
    return split_table(forward), split_table(inverse)


def kernel(n, group, chunks, u_ref, g_ref, h_ref, fwd_hbm, inv_hbm, conv_ref, filt_ref,
           ubuf, gbuf, hbuf, cbuf, fbuf, fwd, inv, tsem, usem, gsem, hsem, osem, fsem,
           su, sg, sh, so, sf):
    me = lax.axis_index("ctx")
    place, layer = me % group, me // group
    layers = n // group
    own = hbuf.shape[2]
    width = own // chunks
    block = inv.shape[0]
    window = 2 * block

    def columns(q, c):
        return pl.ds(pl.multiple_of(q * own + c * width, 128), width)

    def whole(q):
        return pl.ds(pl.multiple_of(q * own, 128), own)

    def send(src, dst, send_sem, recv_sem, device):
        pltpu.make_async_remote_copy(
            src_ref=src, dst_ref=dst, send_sem=send_sem, recv_sem=recv_sem,
            device_id={"ctx": device}, device_id_type=MESH,
        ).start()

    def settle(ref, sem):
        pltpu.make_async_copy(ref, ref, sem).wait()

    barrier = pltpu.get_barrier_semaphore()

    def greet(d, carry):
        pl.semaphore_signal(barrier, inc=1, device_id={"ctx": (me + d) % n}, device_id_type=MESH)
        return carry

    lax.fori_loop(1, n, greet, 0)
    table_f = pltpu.make_async_copy(fwd_hbm, fwd, tsem.at[0])
    table_i = pltpu.make_async_copy(inv_hbm, inv, tsem.at[1])
    table_f.start()
    table_i.start()
    pltpu.make_async_copy(h_ref.at[:, whole(place)], hbuf.at[me], hsem).start()
    for c in range(chunks):
        pltpu.make_async_copy(u_ref.at[:, columns(place, c)], ubuf.at[c, place], usem.at[c]).start()
        pltpu.make_async_copy(g_ref.at[:, columns(place, c)], gbuf.at[c, 0, place], gsem.at[c, 0]).start()
    pl.semaphore_wait(barrier, n - 1)

    def send_taps(d, carry):
        other = (me + d) % n
        send(h_ref.at[:, whole(other % group)], hbuf.at[me], sh, hsem, other)
        return carry

    def send_grads_down(c):
        @pl.when(layer > 0)
        def _():
            for d in range(group):
                q = (place + d) % group
                send(g_ref.at[:, columns(q, c)], gbuf.at[c, 1, place], sg.at[c, 1], gsem.at[c, 1],
                     (layer - 1) * group + q)

    def send_in_layer(c):
        for d in range(1, group):
            q = (place + d) % group
            send(g_ref.at[:, columns(q, c)], gbuf.at[c, 0, place], sg.at[c, 0], gsem.at[c, 0],
                 layer * group + q)
        for d in range(1, group):
            q = (place + d) % group
            send(u_ref.at[:, columns(q, c)], ubuf.at[c, place], su.at[c], usem.at[c],
                 layer * group + q)

    send_grads_down(0)
    lax.fori_loop(1, n, send_taps, 0)
    send_in_layer(0)
    for c in range(1, chunks):
        send_grads_down(c)
        send_in_layer(c)

    def transform(x):
        rows = x.shape[0]
        return (jnp.dot(fwd[:, :rows], x, preferred_element_type=jnp.float32)
                + jnp.dot(fwd[:, window:window + rows], x, preferred_element_type=jnp.float32))

    def correlate(pairs):
        real, imag = 0.0, 0.0
        for first, second in pairs:
            ar, ai, br, bi = first[:block], first[block:], second[:block], second[block:]
            real = real + (ar * br + ai * bi)
            imag = imag + (ai * br - ar * bi)
        joined = jnp.concatenate([real, imag], axis=0)
        high = joined.astype(jnp.bfloat16)
        low = (joined - high.astype(jnp.float32)).astype(jnp.bfloat16)
        return (jnp.dot(inv[:, :window], high, preferred_element_type=jnp.float32)
                + jnp.dot(inv[:, window:], high, preferred_element_type=jnp.float32)
                + jnp.dot(inv[:, :window], low, preferred_element_type=jnp.float32))

    table_f.wait()
    table_i.wait()
    tokens = gbuf.shape[3]
    taps = group * tokens
    rows = hbuf.shape[1]

    def one_chunk(c, carry):
        settle(ubuf.at[c], usem.at[c])
        u = ubuf[c].reshape(taps, width)
        u_spec = [transform(u[b * block:(b + 1) * block]) for b in range(2)]
        settle(gbuf.at[c, 0], gsem.at[c, 0])

        @pl.when(layer < layers - 1)
        def _():
            settle(gbuf.at[c, 1], gsem.at[c, 1])

        @pl.when(layer == layers - 1)
        def _():
            gbuf[c, 1] = jnp.zeros(gbuf.shape[2:], jnp.bfloat16)

        g = gbuf[c].reshape(2 * taps, width)
        g_spec = [transform(g[b * block:b * block + window]) for b in range(3)]
        for m in range(2):
            part = correlate([(g_spec[b + m], u_spec[b]) for b in range(2)])
            fbuf[c, pl.ds(m * (n // 2), n // 2)] = part.reshape(n // 2, rows, width)

        def send_filter(d, inner):
            other = (me + d) % n
            send(fbuf.at[c, other], filt_ref.at[layer, :, columns(place, c)], sf.at[c], fsem, other)
            return inner

        lax.fori_loop(1, n, send_filter, 0)
        pltpu.make_async_copy(fbuf.at[c, me], filt_ref.at[layer, :, columns(place, c)], fsem).start()

        @pl.when(c == 0)
        def _():
            settle(hbuf, hsem)

        h = hbuf[:, :, pl.ds(pl.multiple_of(c * width, 128), width)].astype(jnp.float32)
        h = h.reshape(taps, width).astype(jnp.bfloat16)
        h_spec = [transform(h[b * block:(b + 1) * block]) for b in range(2)]
        for s in range(2):
            part = correlate([(g_spec[s + m], h_spec[m]) for m in range(2)])
            cbuf[c, pl.ds(s * (group // 2), group // 2)] = part.reshape(group // 2, tokens, width)
        for d in range(1, group):
            q = (place + d) % group
            send(cbuf.at[c, q], conv_ref.at[:, columns(place, c)], so.at[c], osem, layer * group + q)
        pltpu.make_async_copy(cbuf.at[c, place], conv_ref.at[:, columns(place, c)], osem).start()
        return carry

    lax.fori_loop(0, chunks, one_chunk, 0)

    settle(conv_ref, osem)
    settle(filt_ref, fsem)
    settle(hbuf.at[pl.ds(0, n - 1)], sh)
    for c in range(chunks):
        settle(ubuf.at[c, pl.ds(0, group - 1)], su.at[c])
        settle(gbuf.at[c, 0, pl.ds(0, group - 1)], sg.at[c, 0])
        settle(cbuf.at[c, pl.ds(0, group - 1)], so.at[c])
        settle(fbuf.at[c, pl.ds(0, n - 1)], sf.at[c])

        @pl.when(layer > 0)
        def _():
            settle(gbuf.at[c, 1], sg.at[c, 1])


def body(n, inputs, out_grad, filter_taps, skip_gain):
    tokens, columns = inputs.shape
    rows = filter_taps.shape[0]
    taps = rows * n
    group = taps // tokens
    own = columns // group
    chunks = 2 if own % 256 == 0 else 1
    width = own // chunks
    block = taps // 2
    forward, inverse = tables(block)
    bf16, f32 = jnp.bfloat16, jnp.float32
    anywhere = pl.BlockSpec(memory_space=pl.ANY)
    dma = pltpu.SemaphoreType.DMA
    conv, filt = pl.pallas_call(
        functools.partial(kernel, n, group, chunks),
        out_shape=(
            jax.ShapeDtypeStruct((tokens, columns), f32),
            jax.ShapeDtypeStruct((n // group, rows, columns), f32),
        ),
        in_specs=[anywhere] * 5,
        out_specs=(anywhere, anywhere),
        scratch_shapes=[
            pltpu.VMEM((chunks, group, tokens, width), bf16),
            pltpu.VMEM((chunks, 2, group, tokens, width), bf16),
            pltpu.VMEM((n, rows, own), bf16),
            pltpu.VMEM((chunks, group, tokens, width), f32),
            pltpu.VMEM((chunks, n, rows, width), f32),
            pltpu.VMEM(forward.shape, bf16),
            pltpu.VMEM(inverse.shape, bf16),
            dma((2,)),
            dma((chunks,)),
            dma((chunks, 2)),
            dma,
            dma,
            dma,
            dma((chunks,)),
            dma((chunks, 2)),
            dma,
            dma((chunks,)),
            dma((chunks,)),
        ],
        compiler_params=pltpu.CompilerParams(
            collective_id=0, has_side_effects=True, vmem_limit_bytes=40 * 1024 * 1024
        ),
        cost_estimate=pl.CostEstimate(
            flops=2 * 5 * taps * taps * own * 4, bytes_accessed=8 * tokens * columns, transcendentals=0
        ),
        name="spectral_exchange",
    )(inputs, out_grad, filter_taps, jnp.asarray(forward), jnp.asarray(inverse))
    input_grad = skip_gain[None, :] * out_grad.astype(f32) + conv
    return input_grad, jnp.sum(filt, axis=0)


def solution(mesh):
    in_specs = (P("ctx", "ch"), P("ctx", "ch"), P("ctx", "ch"), P("ch"))
    out_specs = (P("ctx", "ch"), P("ctx", "ch"))
    return jax.shard_map(functools.partial(body, mesh.shape["ctx"]), mesh=mesh,
                         in_specs=in_specs, out_specs=out_specs, check_vma=False)
```

```python
import functools

import jax
import jax.numpy as jnp
import numpy as np
from jax import lax
from jax.experimental import pallas as pl
from jax.experimental.pallas import tpu as pltpu
from jax.sharding import PartitionSpec as P

MESH = pl.DeviceIdType.MESH


def split_table(table):
    high = table.astype(jnp.bfloat16)
    low = (table - high.astype(np.float64)).astype(jnp.bfloat16)
    return np.concatenate([high, low], axis=1)


def tables(block):
    window = 2 * block
    odd = 2 * np.arange(block, dtype=np.int64)[:, None] + 1
    places = np.arange(window, dtype=np.int64)[None, :]
    angle = np.pi / window * (odd * places % (2 * window)).astype(np.float64)
    forward = np.concatenate([np.cos(angle), -np.sin(angle)], axis=0)
    inverse = forward[:, :block].T / block
    return split_table(forward), split_table(inverse)


def kernel(n, group, chunks, u_ref, g_ref, h_ref, fwd_hbm, inv_hbm, conv_ref, filt_ref,
           ubuf, gbuf, hbuf, cbuf, fbuf, fwd, inv, tsem, usem, gsem, halo, hsem, osem, fsem,
           su, sg, st, sh, so, sf):
    me = lax.axis_index("ctx")
    place, layer = me % group, me // group
    layers, pairs = n // group, group // 2
    pair, core = place // 2, place % 2
    own = hbuf.shape[3]
    width = own // chunks
    block = inv.shape[0]
    window = 2 * block

    def columns(q, c):
        return pl.ds(pl.multiple_of(q * own + c * width, 128), width)

    def whole(q):
        return pl.ds(pl.multiple_of(q * own, 128), own)

    def send(src, dst, send_sem, recv_sem, device):
        pltpu.make_async_remote_copy(
            src_ref=src, dst_ref=dst, send_sem=send_sem, recv_sem=recv_sem,
            device_id={"ctx": device}, device_id_type=MESH,
        ).start()

    def settle(ref, sem):
        pltpu.make_async_copy(ref, ref, sem).wait()

    barrier = pltpu.get_barrier_semaphore()

    def greet(d, carry):
        pl.semaphore_signal(barrier, inc=1, device_id={"ctx": (me + d) % n}, device_id_type=MESH)
        return carry

    lax.fori_loop(1, n, greet, 0)
    table_f = pltpu.make_async_copy(fwd_hbm, fwd, tsem.at[0])
    table_i = pltpu.make_async_copy(inv_hbm, inv, tsem.at[1])
    table_f.start()
    table_i.start()
    pltpu.make_async_copy(h_ref.at[:, whole(place)], hbuf.at[layer, place], hsem.at[layer]).start()
    for c in range(chunks):
        pltpu.make_async_copy(g_ref.at[:, columns(place, c)], gbuf.at[c, 0, pair, core], gsem.at[c, pair]).start()
        pltpu.make_async_copy(u_ref.at[:, columns(place, c)], ubuf.at[c, place], usem.at[c]).start()
    pl.semaphore_wait(barrier, n - 1)

    def send_grads_down(c):
        @pl.when(layer > 0)
        def _():
            for e in range(2):
                q = pair * 2 + (core + e) % 2
                send(g_ref.at[:, columns(q, c)], gbuf.at[c, 1, pair, core], sg.at[c, 1], halo.at[c],
                     (layer - 1) * group + q)

    def send_grads(c):
        for d in range(1, group):
            q = (place + group - d) % group
            send(g_ref.at[:, columns(q, c)], gbuf.at[c, 0, pair, core], sg.at[c, 0], gsem.at[c, pair],
                 layer * group + q)

    def send_inputs(c):
        for d in range(1, group):
            q = (place + d) % group
            send(u_ref.at[:, columns(q, c)], ubuf.at[c, place], su.at[c], usem.at[c],
                 layer * group + q)

    def forward_grads(c):
        for d in range(1, pairs):
            other = (pair + d) % pairs
            settle(gbuf.at[c, 0, other], gsem.at[c, other])

            @pl.when(layer > 0)
            def _():
                send(gbuf.at[c, 0, other], gbuf.at[c, 1, other], sg.at[c, 1], halo.at[c], me - group)

    def pass_taps(slot, way, step):
        send(hbuf.at[slot], hbuf.at[slot], sh.at[way, step], hsem.at[slot], me + (1 - 2 * way) * group)

    for d in range(1, group):
        q = (place + d) % group
        send(h_ref.at[:, whole(q)], hbuf.at[layer, place], st, hsem.at[layer], layer * group + q)
    for c in range(chunks):
        send_grads_down(c)
        send_grads(c)
    for c in range(chunks):
        send_inputs(c)
    settle(hbuf.at[layer], hsem.at[layer])

    @pl.when(layer > 0)
    def _():
        pass_taps(layer, 1, 0)

    @pl.when(layer < layers - 1)
    def _():
        pass_taps(layer, 0, 0)

    for c in range(chunks):
        forward_grads(c)

    def forward_taps(step, carry):
        @pl.when((layer >= step) & (layer < layers - 1))
        def _():
            settle(hbuf.at[layer - step], hsem.at[layer - step])
            pass_taps(layer - step, 0, step)

        @pl.when((layer + step < layers) & (layer > 0))
        def _():
            settle(hbuf.at[layer + step], hsem.at[layer + step])
            pass_taps(layer + step, 1, step)

        return carry

    lax.fori_loop(1, layers, forward_taps, 0)

    def last_taps(step, carry):
        @pl.when(layer == layers - 1)
        def _():
            settle(hbuf.at[layers - 1 - step], hsem.at[layers - 1 - step])

        @pl.when(layer == 0)
        def _():
            settle(hbuf.at[step], hsem.at[step])

        return carry

    def sent_taps(step, carry):
        @pl.when((layer >= step) & (layer < layers - 1))
        def _():
            settle(hbuf.at[0], sh.at[0, step])

        @pl.when((layer + step < layers) & (layer > 0))
        def _():
            settle(hbuf.at[0], sh.at[1, step])

        return carry

    def transform(x):
        rows = x.shape[0]
        return (jnp.dot(fwd[:, :rows], x, preferred_element_type=jnp.float32)
                + jnp.dot(fwd[:, window:window + rows], x, preferred_element_type=jnp.float32))

    def correlate(pairs):
        real, imag = 0.0, 0.0
        for first, second in pairs:
            ar, ai, br, bi = first[:block], first[block:], second[:block], second[block:]
            real = real + (ar * br + ai * bi)
            imag = imag + (ai * br - ar * bi)
        joined = jnp.concatenate([real, imag], axis=0)
        high = joined.astype(jnp.bfloat16)
        low = (joined - high.astype(jnp.float32)).astype(jnp.bfloat16)
        return (jnp.dot(inv[:, :window], high, preferred_element_type=jnp.float32)
                + jnp.dot(inv[:, window:], high, preferred_element_type=jnp.float32)
                + jnp.dot(inv[:, :window], low, preferred_element_type=jnp.float32))

    table_f.wait()
    table_i.wait()
    tokens = ubuf.shape[2]
    taps = group * tokens
    rows = hbuf.shape[2]

    def one_chunk(c, carry):
        settle(ubuf.at[c], usem.at[c])
        u = ubuf[c].reshape(taps, width)
        u_spec = [transform(u[b * block:(b + 1) * block]) for b in range(2)]
        settle(gbuf.at[c, 0, pair], gsem.at[c, pair])

        @pl.when(layer < layers - 1)
        def _():
            settle(gbuf.at[c, 1], halo.at[c])

        @pl.when(layer == layers - 1)
        def _():
            gbuf[c, 1] = jnp.zeros(gbuf.shape[2:], jnp.bfloat16)

        g = gbuf[c].reshape(2 * taps, width)
        g_spec = [transform(g[b * block:b * block + window]) for b in range(3)]
        for m in range(2):
            part = correlate([(g_spec[b + m], u_spec[b]) for b in range(2)])
            fbuf[c, pl.ds(m * (n // 2), n // 2)] = part.reshape(n // 2, rows, width)

        def send_filter(d, inner):
            other = (me + d) % n
            send(fbuf.at[c, other], filt_ref.at[layer, :, columns(place, c)], sf.at[c], fsem, other)
            return inner

        lax.fori_loop(1, n, send_filter, 0)
        pltpu.make_async_copy(fbuf.at[c, me], filt_ref.at[layer, :, columns(place, c)], fsem).start()

        @pl.when(c == 0)
        def _():
            lax.fori_loop(1, layers, last_taps, 0)

        h = hbuf[:, :, :, pl.ds(pl.multiple_of(c * width, 128), width)].astype(jnp.float32)
        h = h.reshape(taps, width).astype(jnp.bfloat16)
        h_spec = [transform(h[b * block:(b + 1) * block]) for b in range(2)]
        for s in range(2):
            part = correlate([(g_spec[s + m], h_spec[m]) for m in range(2)])
            cbuf[c, pl.ds(s * (group // 2), group // 2)] = part.reshape(group // 2, tokens, width)
        for d in range(1, group):
            q = (place + d) % group
            send(cbuf.at[c, q], conv_ref.at[:, columns(place, c)], so.at[c], osem, layer * group + q)
        pltpu.make_async_copy(cbuf.at[c, place], conv_ref.at[:, columns(place, c)], osem).start()
        return carry

    lax.fori_loop(0, chunks, one_chunk, 0)

    settle(conv_ref, osem)
    settle(filt_ref, fsem)
    settle(hbuf.at[0, pl.ds(0, group - 1)], st)
    lax.fori_loop(0, layers, sent_taps, 0)
    for c in range(chunks):
        settle(ubuf.at[c, pl.ds(0, group - 1)], su.at[c])
        settle(ubuf.at[c, pl.ds(0, group - 1)], sg.at[c, 0])
        settle(cbuf.at[c, pl.ds(0, group - 1)], so.at[c])
        settle(fbuf.at[c, pl.ds(0, n - 1)], sf.at[c])

        @pl.when(layer > 0)
        def _():
            settle(gbuf.at[c, 1], sg.at[c, 1])


def body(n, inputs, out_grad, filter_taps, skip_gain):
    tokens, columns = inputs.shape
    rows = filter_taps.shape[0]
    taps = rows * n
    group = taps // tokens
    own = columns // group
    chunks = 2 if own % 256 == 0 else 1
    width = own // chunks
    block = taps // 2
    forward, inverse = tables(block)
    bf16, f32 = jnp.bfloat16, jnp.float32
    anywhere = pl.BlockSpec(memory_space=pl.ANY)
    dma = pltpu.SemaphoreType.DMA
    conv, filt = pl.pallas_call(
        functools.partial(kernel, n, group, chunks),
        out_shape=(
            jax.ShapeDtypeStruct((tokens, columns), f32),
            jax.ShapeDtypeStruct((n // group, rows, columns), f32),
        ),
        in_specs=[pl.BlockSpec(memory_space=pltpu.HBM)] * 5,
        out_specs=(anywhere, anywhere),
        scratch_shapes=[
            pltpu.VMEM((chunks, group, tokens, width), bf16),
            pltpu.VMEM((chunks, 2, group // 2, 2, tokens, width), bf16),
            pltpu.VMEM((n // group, group, rows, own), bf16),
            pltpu.VMEM((chunks, group, tokens, width), f32),
            pltpu.VMEM((chunks, n, rows, width), f32),
            pltpu.VMEM(forward.shape, bf16),
            pltpu.VMEM(inverse.shape, bf16),
            dma((2,)),
            dma((chunks,)),
            dma((chunks, group // 2)),
            dma((chunks,)),
            dma((n // group,)),
            dma,
            dma,
            dma((chunks,)),
            dma((chunks, 2)),
            dma,
            dma((2, n // group)),
            dma((chunks,)),
            dma((chunks,)),
        ],
        compiler_params=pltpu.CompilerParams(
            collective_id=0, has_side_effects=True, vmem_limit_bytes=63 * 1024 * 1024
        ),
        cost_estimate=pl.CostEstimate(
            flops=2 * 5 * taps * taps * own * 4, bytes_accessed=8 * tokens * columns, transcendentals=0
        ),
        name="spectral_exchange",
    )(inputs, out_grad, filter_taps, jnp.asarray(forward), jnp.asarray(inverse))
    input_grad = skip_gain[None, :] * out_grad.astype(f32) + conv
    return input_grad, jnp.sum(filt, axis=0)


def solution(mesh):
    in_specs = (P("ctx", "ch"), P("ctx", "ch"), P("ctx", "ch"), P("ch"))
    out_specs = (P("ctx", "ch"), P("ctx", "ch"))
    return jax.shard_map(functools.partial(body, mesh.shape["ctx"]), mesh=mesh,
                         in_specs=in_specs, out_specs=out_specs, check_vma=False)
```
